32 devices in a mesh: row: 4 (over y, core), col: 8 (over z, x).
Axes of the slice: x: 2, y: 2, z: 4, core: 2. Of those that a mesh axis runs over, the one named last changes fastest.
Arguments:
- weights: float32 [40, 2048, 4096], P(None, 'row', 'col'), may hold values from -0.006214806 to 0.006214806
- pool: float32 [12, 2048, 4096], P(None, 'row', 'col'), may hold values from -6 to 6
- desired: float32 [12, 8], replicated, may hold values from -6 to 6
- plan: int32 [2, 16], replicated, may hold values from 0 to 11
- beam_ref: int32 [40], replicated, may hold values from 0 to 7
- step_size: float32 [40], replicated, may hold values from 0.2 to 0.8
- smoothing: float32 [40], replicated, may hold values from 0.05 to 0.2
- active: int32 [40], replicated, may hold values from 1 to 2
Outputs:
- final_weights: float32 [40, 2048, 4096], P(None, 'row', 'col')
- errors: float32 [2, 40, 16], replicated
The draws below stay inside these ranges and needn't reach their ends.
Inputs may be any that keep to these rules, and one draw needn't show every extreme that they name: `plan`: indices of recorded snapshots. `beam_ref`: indices of reference signals.
All inputs are finite; a program needn't handle non-finite values.
Results may differ from the reference program's by a relative error of at most 0.00017.
Values sent between devices are 32-bit elements; how exact they have to be, the bound alone decides.
A program may use at most 384 MiB of HBM per device.

```python
import math
import jax
import jax.numpy as jnp
from jax import lax

NR = 2048
NC = 4096
B = 40
S = 16
POOL = 12
REFS = 8
ITERS = 2


def set_ends(values, stream_key, least, high):
    longest = values.shape.index(max(values.shape))
    spots = []
    for shift in (0, 1):
        where = [jax.random.randint(jax.random.fold_in(stream_key, axis), (), 0, length) for axis, length in enumerate(values.shape)]
        where[longest] = (where[longest] + shift) % values.shape[longest]
        spots.append(tuple(where))
    return values.at[spots[0]].set(least).at[spots[1]].set(high)


def levels(own_key, extent, pieces, least, top_value):
    factor_of = 1.0
    for dim, parts in pieces:
        draws = jax.random.uniform(jax.random.fold_in(jax.random.fold_in(own_key, 6), dim), (parts,), jnp.float32, least / len(pieces), top_value / len(pieces))
        factor_of = factor_of * jnp.repeat(jnp.exp(draws), extent[dim] // parts).reshape((-1,) + (1,) * (len(extent) - 1 - dim))
    return factor_of


def noise(stream_key, shape, width, bound, cuts=(), dtype=jnp.bfloat16):
    values = width * jax.random.normal(stream_key, shape, jnp.float32)
    if cuts:
        values = values * levels(stream_key, shape, cuts, -0.22, 0.18)
    return jnp.clip(values, -bound, bound).astype(dtype)


def setup_inputs(seed: int = 0) -> dict:
    key_of = jax.random.split(jax.random.key(seed), 9)
    weights = noise(key_of[0], (B, NR, NC), (3.0 / (NR * NC) ** 0.5), 0.006214806, ((1, 4), (2, 8)), jnp.float32)
    pool = noise(key_of[1], (POOL, NR, NC), 1.0, 6.0, ((1, 4), (2, 8)), jnp.float32)
    desired = noise(key_of[2], (POOL, REFS), 1.0, 6.0, (), jnp.float32)
    plan = set_ends(jax.random.randint(key_of[3], (ITERS, S), 0, POOL), jax.random.fold_in(key_of[3], 1), 0, POOL - 1).astype(jnp.int32)
    beam_ref = set_ends(jax.random.randint(key_of[4], (B,), 0, REFS), jax.random.fold_in(key_of[4], 1), 0, REFS - 1).astype(jnp.int32)
    step_size = jnp.clip(jnp.exp(jax.random.uniform(key_of[5], (B,), jnp.float32, math.log(0.2), math.log(0.8))), 0.2, 0.8)
    smoothing = jnp.clip(jax.random.uniform(key_of[6], (B,), jnp.float32, 0.05, 0.2), 0.05, 0.2)
    active = set_ends(jax.random.randint(key_of[7], (B,), 1, ITERS + 1), jax.random.fold_in(key_of[7], 1), 1, ITERS).astype(jnp.int32)
    return {"weights": weights, "pool": pool, "desired": desired, "plan": plan, "beam_ref": beam_ref, "step_size": step_size, "smoothing": smoothing, "active": active}


def laplace(field):
    padded = jnp.pad(field, ((0, 0), (1, 1), (1, 1)))
    return padded[:, 2:, 1:-1] + padded[:, :-2, 1:-1] + padded[:, 1:-1, 2:] + padded[:, 1:-1, :-2] - 4.0 * field

def reference(weights, pool, desired, plan, beam_ref, step_size, smoothing, active):
    scale = 1.0 / math.sqrt(NR * NC)
    current = weights
    history = []
    for step in range(ITERS):
        snaps = jnp.take(pool, plan[step], axis=0).reshape(S, -1)
        beam_out = jnp.dot(current.reshape(B, -1), snaps.T, precision=lax.Precision.HIGHEST) * scale
        target = jnp.take(desired, plan[step], axis=0)[:, beam_ref].T
        error = target - beam_out
        history.append(error)
        grad = jnp.dot(error, snaps, precision=lax.Precision.HIGHEST).reshape(current.shape)
        live = (active > step).astype(jnp.float32)[:, None, None]
        update = step_size[:, None, None] * scale * grad + smoothing[:, None, None] * laplace(current)
        current = current + live * update
    return (current, jnp.stack(history))
```

```python
import functools
import math

import jax
import jax.numpy as jnp
from jax import lax
from jax.experimental import pallas as pl
from jax.experimental.pallas import tpu as pltpu
from jax.sharding import PartitionSpec as P

F32 = jnp.float32
BF16 = jnp.bfloat16
NT = (((1,), (1,)), ((), ()))
LIMIT = 56 * 1024 * 1024


def split(x):
    hi = x.astype(BF16)
    lo = (x - hi.astype(F32)).astype(BF16)
    return hi, lo


def neighbours(x, axis):
    size = x.shape[axis]
    return pltpu.roll(x, 1, axis) + pltpu.roll(x, size - 1, axis)


def laplacian(x):
    return neighbours(x, 0) + neighbours(x, 1) - 4.0 * x


def one_hot(rows, cols, hit):
    r = lax.broadcasted_iota(jnp.int32, (rows, cols), 0)
    c = lax.broadcasted_iota(jnp.int32, (rows, cols), 1)
    return jnp.where(hit(r, c), 1.0, 0.0).astype(F32)


def moments_kernel(w_ref, x_ref, xp_ref, xn_ref, xt_ref, xb_ref, xe_ref, out_ref, lx_ref, el_ref, er_ref, acc_ref):
    i, last = pl.program_id(0), pl.num_programs(0) - 1
    beams, rows, cols = w_ref.shape
    pool = x_ref.shape[0]

    @pl.when(i == 0)
    def _():
        acc_ref[...] = jnp.zeros_like(acc_ref)

    for p in range(pool):
        above = jnp.where(i == 0, xt_ref[p], xp_ref[p])
        below = jnp.where(i == last, xb_ref[p], xn_ref[p])
        cur = x_ref[p]
        tall = jnp.concatenate([above, cur, below], axis=0)
        wide = jnp.concatenate([cur, xe_ref[p]], axis=1)
        lx_ref[p] = neighbours(tall, 0)[8 : rows + 8] + neighbours(wide, 1)[:, :cols] - 4.0 * cur

    for g in range(rows // 8):
        part = pl.ds(8 * g, 8)
        wg = w_ref[:, part, :].reshape(beams * 8, cols)
        xg = x_ref[:, part, :].reshape(pool * 8, cols)
        lg = lx_ref[:, part, :].reshape(pool * 8, cols)
        lh, ll = split(jnp.concatenate([wg, xg], axis=0))
        rh, rl = split(jnp.concatenate([xg, lg], axis=0))
        left = jnp.concatenate([lh, ll, lh], axis=1)
        right = jnp.concatenate([rh, rh, rl], axis=1)
        acc_ref[...] += lax.dot_general(left, right, NT, preferred_element_type=F32)

    def edge(tile, lane):
        pick = one_hot(8, 128, lambda r, c: c == r + lane).astype(BF16)
        h, m = split(tile)
        l = (tile - h.astype(F32) - m.astype(F32)).astype(BF16)
        return (
            lax.dot_general(pick, h, NT, preferred_element_type=F32)
            + lax.dot_general(pick, m, NT, preferred_element_type=F32)
            + lax.dot_general(pick, l, NT, preferred_element_type=F32)
        )[:2]

    el_ref[0] = edge(w_ref[:, :, :128].reshape(beams * rows, 128), 0)
    er_ref[0] = edge(w_ref[:, :, cols - 128 :].reshape(beams * rows, 128), 126)

    @pl.when(i == last)
    def _():
        n, m = acc_ref.shape
        kept = acc_ref[...] * one_hot(n, m, lambda r, c: r % 8 == c % 8)
        fold = one_hot(m, 128, lambda r, c: r // 8 == c)
        gather = one_hot(out_ref.shape[0], n, lambda r, c: c // 8 == r)
        half = jnp.dot(kept, fold, precision=lax.Precision.HIGHEST, preferred_element_type=F32)
        out_ref[...] = jnp.dot(gather, half, precision=lax.Precision.HIGHEST, preferred_element_type=F32)


def update_kernel(
    a_ref, b_ref, flag_ref, w_ref, wp_ref, wn_ref, wt_ref, wb_ref, halo_ref, x_ref, lx_ref, mix_ref,
    out_ref, tile_ref, mask_ref
):
    i, last = pl.program_id(0), pl.num_programs(0) - 1
    beams, rows, cols = w_ref.shape
    pool = x_ref.shape[0]
    width = cols + 128

    def make_tile(j):
        raw = halo_ref[j]
        h = raw.astype(BF16).astype(F32)
        m = (raw - h).astype(BF16).astype(F32)
        l = raw - h - m
        stack = jnp.concatenate([h, m, l, jnp.zeros_like(h)], axis=0)
        r = lax.broadcasted_iota(jnp.int32, (16, 128), 0)
        c = lax.broadcasted_iota(jnp.int32, (16, 128), 1)
        k = r % 4
        spot = jnp.where(k < 2, k + 126, k - 2)
        place = jnp.where((c == spot) & (r < 12), 1.0, 0.0).astype(BF16)
        tile = jnp.dot(stack.T.astype(BF16), place, preferred_element_type=F32)
        tile_ref[j % 3] = tile.reshape(beams, rows, 128)

    @pl.when(i == 0)
    def _():
        make_tile(0)
        make_tile(1)

    make_tile(i + 2)

    r = lax.broadcasted_iota(jnp.int32, (rows + 16, width), 0)
    c = lax.broadcasted_iota(jnp.int32, (rows + 16, width), 1)
    mask = jnp.ones((rows + 16, width), F32)
    mask = jnp.where((r < 8) & (i == 0), flag_ref[0], mask)
    mask = jnp.where((r >= rows + 8) & (i == last), flag_ref[1], mask)
    mask = mask * jnp.where(c >= cols + 64, flag_ref[2], 1.0)
    mask_ref[...] = mask * jnp.where((c >= cols) & (c < cols + 64), flag_ref[3], 1.0)

    for g in range(rows // 8):
        part = pl.ds(8 * g, 8)
        xg = x_ref[:, part, :].reshape(pool * 8, cols)
        lg = lx_ref[:, part, :].reshape(pool * 8, cols)
        rh, rl = split(jnp.concatenate([xg, lg], axis=0))
        full = jnp.concatenate([rh, rl, rh], axis=0)
        mixed = jnp.dot(mix_ref[...], full, preferred_element_type=F32)
        out_ref[:, part, :] = mixed.reshape(beams, 8, cols)

    before, here, after = lax.rem(i, 3), lax.rem(i + 1, 3), lax.rem(i + 2, 3)

    def beam(n, carry):
        cur = w_ref[n]
        a, b = a_ref[n], b_ref[n]

        def field():
            above = jnp.where(i == 0, wt_ref[n], wp_ref[n])
            below = jnp.where(i == last, wb_ref[n], wn_ref[n])
            main = jnp.concatenate([above, cur, below], axis=0)
            side = jnp.concatenate(
                [tile_ref[before, n, rows - 8 :], tile_ref[here, n], tile_ref[after, n, :8]], axis=0
            )
            return jnp.concatenate([main, side], axis=1)

        @pl.when(b == 0.0)
        def _():
            out_ref[n] += cur + a * laplacian(field())[8 : rows + 8, :cols]

        @pl.when(b != 0.0)
        def _():
            wide = field()
            q = a * wide + b * (laplacian(wide) * mask_ref[...])
            out_ref[n] += cur + laplacian(q)[8 : rows + 8, :cols]

        return carry

    lax.fori_loop(0, beams, beam, 0)


def shift_pair(first, final, axis):
    count = lax.axis_size(axis)
    up = [(i, i + 1) for i in range(count - 1)]
    down = [(i + 1, i) for i in range(count - 1)]
    return lax.ppermute(final, axis, up), lax.ppermute(first, axis, down)


def total(value):
    for axis in ("row", "col"):
        count = lax.axis_size(axis)
        if count & (count - 1):
            value = lax.psum(value, axis)
            continue
        hop = 1
        while hop < count:
            value = value + lax.ppermute(value, axis, [(i, i ^ hop) for i in range(count)])
            hop *= 2
    return value


def body(rows, weights, pool, desired, plan, beam_ref, step_size, smoothing, active):
    beams, height, cols = weights.shape
    count = pool.shape[0]
    blocks = height // rows
    eighths = rows // 8
    row_n, col_n = lax.axis_size("row"), lax.axis_size("col")
    row_i, col_i = lax.axis_index("row"), lax.axis_index("col")
    scale = 1.0 / math.sqrt(height * row_n * cols * col_n)
    high = lax.Precision.HIGHEST

    xt, xb = shift_pair(pool[:, :8], pool[:, -8:], "row")
    xl, xr = shift_pair(pool[:, :, 0], pool[:, :, -1], "col")
    lane = jnp.arange(128)[None, None, :]
    xe = jnp.where(lane == 0, xr[:, :, None], jnp.where(lane == 127, xl[:, :, None], 0.0))
    wt, wb = shift_pair(weights[:, :8], weights[:, -8:], "row")

    def block(n, r=rows, w=cols):
        return pl.BlockSpec((n, r, w), lambda i: (0, i, 0))

    def previous(n):
        return pl.BlockSpec((n, 8, cols), lambda i: (0, jnp.maximum(i * eighths - 1, 0), 0))

    def following(n):
        return pl.BlockSpec((n, 8, cols), lambda i: (0, jnp.minimum((i + 1) * eighths, blocks * eighths - 1), 0))

    def whole(*shape):
        return pl.BlockSpec(shape, lambda i: (0,) * len(shape))

    edges = pl.BlockSpec((1, 2, beams * rows), lambda i: (i, 0, 0))
    planes = -(-(beams + count) // 8) * 8
    sums, lx, first, final = pl.pallas_call(
        moments_kernel,
        grid=(blocks,),
        in_specs=[block(beams), block(count), previous(count), following(count), whole(count, 8, cols),
                  whole(count, 8, cols), block(count, rows, 128)],
        out_specs=[whole(planes, 128), block(count), edges, edges],
        out_shape=[
            jax.ShapeDtypeStruct((planes, 128), F32),
            jax.ShapeDtypeStruct(pool.shape, F32),
            jax.ShapeDtypeStruct((blocks, 2, beams * rows), F32),
            jax.ShapeDtypeStruct((blocks, 2, beams * rows), F32),
        ],
        scratch_shapes=[pltpu.VMEM(((beams + count) * 8, 2 * count * 8), F32)],
        compiler_params=pltpu.CompilerParams(vmem_limit_bytes=LIMIT),
        cost_estimate=pl.CostEstimate(flops=10**10, bytes_accessed=10**8, transcendentals=0),
        name="moments",
    )(weights, pool, pool, pool, xt, xb, xe)

    left, right = shift_pair(first, final, "col")
    halo = jnp.concatenate([left, right], axis=1)
    top, bottom = shift_pair(halo[:1], halo[-1:], "row")
    halo = jnp.concatenate([top, halo, bottom], axis=0)

    sums = total(sums)
    gram, lapped, cross = sums[:beams, :count], sums[:beams, count : 2 * count], sums[beams : beams + count, :count]
    refs = desired.shape[1]
    pick = (beam_ref[:, None] == jnp.arange(refs, dtype=jnp.int32)[None, :]).astype(F32)
    targets = jnp.dot(pick, desired.T, precision=high)
    rate = (step_size * scale)[:, None]
    chosen = [(plan[t][None, :] == jnp.arange(count, dtype=jnp.int32)[:, None]).astype(F32) for t in range(2)]
    live = [(active > t).astype(F32)[:, None] for t in range(2)]
    s0, s1 = (live[t] * smoothing[:, None] for t in range(2))

    error0 = jnp.dot(targets - scale * gram, chosen[0], precision=high)
    c0 = live[0] * rate * jnp.dot(error0, chosen[0].T, precision=high)
    later = gram + s0 * lapped + jnp.dot(c0, cross, precision=high)
    error1 = jnp.dot(targets - scale * later, chosen[1], precision=high)
    c1 = live[1] * rate * jnp.dot(error1, chosen[1].T, precision=high)

    mix = jnp.concatenate([c0 + c1, s1 * c0], axis=1)
    mix = (mix[:, None, :, None] * jnp.eye(8, dtype=F32)[None, :, None, :]).reshape(beams * 8, 2 * count * 8)
    mix_hi = lax.reduce_precision(mix, 8, 7)
    mix_lo = (mix - mix_hi).astype(BF16)
    mix_hi = mix_hi.astype(BF16)
    mix = jnp.concatenate([mix_hi, mix_hi, mix_lo], axis=1)
    flags = jnp.stack([row_i > 0, row_i < row_n - 1, col_i > 0, col_i < col_n - 1]).astype(F32)

    smem = pl.BlockSpec(memory_space=pltpu.SMEM)
    out = pl.pallas_call(
        update_kernel,
        grid=(blocks,),
        in_specs=[smem, smem, smem, block(beams), previous(beams), following(beams), whole(beams, 8, cols),
                  whole(beams, 8, cols), whole(blocks + 2, 4, beams * rows), block(count), block(count),
                  whole(beams * 8, 6 * count * 8)],
        out_specs=block(beams),
        out_shape=jax.ShapeDtypeStruct(weights.shape, F32),
        scratch_shapes=[pltpu.VMEM((3, beams, rows, 128), F32), pltpu.VMEM((rows + 16, cols + 128), F32)],
        compiler_params=pltpu.CompilerParams(vmem_limit_bytes=LIMIT),
        cost_estimate=pl.CostEstimate(flops=10**10, bytes_accessed=10**8, transcendentals=0),
        name="update",
    )((s0 + s1)[:, 0], (s0 * s1)[:, 0], flags, weights, weights, weights, wt, wb, halo, pool, lx, mix)
    return out, jnp.stack([error0, error1])


def solution(mesh):
    in_specs = (P(None, "row", "col"), P(None, "row", "col"), P(), P(), P(), P(), P(), P())
    out_specs = (P(None, "row", "col"), P())
    return jax.shard_map(functools.partial(body, 32), mesh=mesh, in_specs=in_specs, out_specs=out_specs, check_vma=False)
```

```python
import functools
import math

import jax
import jax.numpy as jnp
from jax import lax
from jax.experimental import pallas as pl
from jax.experimental.pallas import tpu as pltpu
from jax.sharding import PartitionSpec as P

F32 = jnp.float32
BF16 = jnp.bfloat16
NT = (((1,), (1,)), ((), ()))
LIMIT = 56 * 1024 * 1024


def split(x):
    hi = x.astype(BF16)
    lo = (x - hi.astype(F32)).astype(BF16)
    return hi, lo


def neighbours(x, axis):
    size = x.shape[axis]
    return pltpu.roll(x, 1, axis) + pltpu.roll(x, size - 1, axis)


def one_hot(rows, cols, hit):
    r = lax.broadcasted_iota(jnp.int32, (rows, cols), 0)
    c = lax.broadcasted_iota(jnp.int32, (rows, cols), 1)
    return jnp.where(hit(r, c), 1.0, 0.0).astype(F32)


def moments_kernel(w_ref, x_ref, xp_ref, xn_ref, xt_ref, xb_ref, xe_ref, out_ref, lx_ref, el_ref, er_ref, acc_ref):
    i, last = pl.program_id(0), pl.num_programs(0) - 1
    beams, rows, cols = w_ref.shape
    pool = x_ref.shape[0]

    @pl.when(i == 0)
    def _():
        acc_ref[...] = jnp.zeros_like(acc_ref)

    for p in range(pool):
        above = jnp.where(i == 0, xt_ref[p], xp_ref[p])
        below = jnp.where(i == last, xb_ref[p], xn_ref[p])
        cur = x_ref[p]
        tall = jnp.concatenate([above, cur, below], axis=0)
        wide = jnp.concatenate([cur, xe_ref[p]], axis=1)
        lx_ref[p] = neighbours(tall, 0)[8 : rows + 8] + neighbours(wide, 1)[:, :cols] - 4.0 * cur

    for g in range(rows // 8):
        part = pl.ds(8 * g, 8)
        wg = w_ref[:, part, :].reshape(beams * 8, cols)
        xg = x_ref[:, part, :].reshape(pool * 8, cols)
        lg = lx_ref[:, part, :].reshape(pool * 8, cols)
        lh, ll = split(jnp.concatenate([wg, xg], axis=0))
        rh, rl = split(jnp.concatenate([xg, lg], axis=0))
        left = jnp.concatenate([lh, ll, lh], axis=1)
        right = jnp.concatenate([rh, rh, rl], axis=1)
        acc_ref[...] += lax.dot_general(left, right, NT, preferred_element_type=F32)

    def edge(tile, lane):
        pick = one_hot(8, 128, lambda r, c: c == r + lane).astype(BF16)
        h, m = split(tile)
        l = (tile - h.astype(F32) - m.astype(F32)).astype(BF16)
        return (
            lax.dot_general(pick, h, NT, preferred_element_type=F32)
            + lax.dot_general(pick, m, NT, preferred_element_type=F32)
            + lax.dot_general(pick, l, NT, preferred_element_type=F32)
        )[:2]

    el_ref[0] = edge(w_ref[:, :, :128].reshape(beams * rows, 128), 0)
    er_ref[0] = edge(w_ref[:, :, cols - 128 :].reshape(beams * rows, 128), 126)

    @pl.when(i == last)
    def _():
        n, m = acc_ref.shape
        kept = acc_ref[...] * one_hot(n, m, lambda r, c: r % 8 == c % 8)
        fold = one_hot(m, 128, lambda r, c: r // 8 == c)
        gather = one_hot(out_ref.shape[0], n, lambda r, c: c // 8 == r)
        half = jnp.dot(kept, fold, precision=lax.Precision.HIGHEST, preferred_element_type=F32)
        out_ref[...] = jnp.dot(gather, half, precision=lax.Precision.HIGHEST, preferred_element_type=F32)


def update_kernel(
    a_ref, b_ref, flag_ref, w_ref, wp_ref, wn_ref, wt_ref, wb_ref, halo_ref, x_ref, lx_ref, coef_ref,
    out_ref, tile_ref, mask_ref, mix_ref, s_ref, q_ref
):
    i, last = pl.program_id(0), pl.num_programs(0) - 1
    beams, rows, cols = w_ref.shape
    pool = x_ref.shape[0]
    tiles = cols // 128

    def make_tile(j):
        raw = halo_ref[j]
        h = raw.astype(BF16).astype(F32)
        m = (raw - h).astype(BF16).astype(F32)
        l = raw - h - m
        stack = jnp.concatenate([h, m, l, jnp.zeros_like(h)], axis=0)
        r = lax.broadcasted_iota(jnp.int32, (16, 128), 0)
        c = lax.broadcasted_iota(jnp.int32, (16, 128), 1)
        k = r % 4
        spot = jnp.where(k < 2, k + 126, k - 2)
        place = jnp.where((c == spot) & (r < 12), 1.0, 0.0).astype(BF16)
        tile = jnp.dot(stack.T.astype(BF16), place, preferred_element_type=F32)
        tile_ref[j % 3] = tile.reshape(beams, rows, 128)

    @pl.when(i == 0)
    def _():
        make_tile(0)
        make_tile(1)
        n, m = beams * 8, 2 * pool * 8
        down = one_hot(n, beams, lambda r, c: r // 8 == c)
        along = one_hot(2 * pool, m, lambda r, c: r == c // 8)
        full = jnp.dot(down, coef_ref[...], precision=lax.Precision.HIGHEST, preferred_element_type=F32)
        full = jnp.dot(full, along, precision=lax.Precision.HIGHEST, preferred_element_type=F32)
        high, low = split(full * one_hot(n, m, lambda r, c: r % 8 == c % 8))
        mix_ref[...] = jnp.concatenate([high, high, low], axis=1)

    make_tile(i + 2)

    r = lax.broadcasted_iota(jnp.int32, (rows + 8, 128), 0)
    c = lax.broadcasted_iota(jnp.int32, (rows + 8, 128), 1)
    mask = jnp.where((r == 0) & (i == 0), flag_ref[0], 1.0)
    mask = jnp.where((r == rows + 1) & (i == last), flag_ref[1], mask)
    mask_ref[0] = mask
    mask_ref[1] = mask * jnp.where(c >= 64, flag_ref[2], flag_ref[3])

    for g in range(rows // 8):
        part = pl.ds(8 * g, 8)
        xg = x_ref[:, part, :].reshape(pool * 8, cols)
        lg = lx_ref[:, part, :].reshape(pool * 8, cols)
        rh, rl = split(jnp.concatenate([xg, lg], axis=0))
        full = jnp.concatenate([rh, rl, rh], axis=0)
        mixed = jnp.dot(mix_ref[...], full, preferred_element_type=F32)
        out_ref[:, part, :] = mixed.reshape(beams, 8, cols)

    before, here, after = lax.rem(i, 3), lax.rem(i + 1, 3), lax.rem(i + 2, 3)

    def across(parts, count):
        lane = lax.broadcasted_iota(jnp.int32, parts[0].shape, 1)
        one = [pltpu.roll(v, 1, 1) for v in parts]
        two = [pltpu.roll(v, 127, 1) for v in parts]
        n = len(parts)
        return [
            jnp.where(lane == 0, one[k - 1], one[k]) + jnp.where(lane == 127, two[(k + 1) % n], two[k])
            for k in range(count)
        ]

    def lap_rows(ref, start, size, count):
        mid = [ref[k, pl.ds(start, size)] for k in range(tiles + 1)]
        side = across(mid, count)
        laps = [
            ref[k, pl.ds(start - 1, size)] + ref[k, pl.ds(start + 1, size)] + side[k] - 4.0 * mid[k]
            for k in range(count)
        ]
        return mid, laps

    def beam(n, carry):
        a, b = a_ref[n], b_ref[n]
        for k in range(tiles):
            lanes = pl.ds(128 * k, 128)
            s_ref[k, pl.ds(0, 8)] = jnp.where(i == 0, wt_ref[n, :, lanes], wp_ref[n, :, lanes])
            s_ref[k, pl.ds(8, rows)] = w_ref[n, :, lanes]
            s_ref[k, pl.ds(rows + 8, 8)] = jnp.where(i == last, wb_ref[n, :, lanes], wn_ref[n, :, lanes])
        s_ref[tiles, pl.ds(0, 8)] = tile_ref[before, n, pl.ds(rows - 8, 8)]
        s_ref[tiles, pl.ds(8, rows)] = tile_ref[here, n]
        s_ref[tiles, pl.ds(rows + 8, 8)] = tile_ref[after, n, pl.ds(0, 8)]

        @pl.when(b == 0.0)
        def _():
            for t in range(0, rows, 16):
                mid, laps = lap_rows(s_ref, 8 + t, 16, tiles)
                for k in range(tiles):
                    spot = (n, pl.ds(t, 16), pl.ds(128 * k, 128))
                    out_ref[spot] = out_ref[spot] + mid[k] + a * laps[k]

        @pl.when(b != 0.0)
        def _():
            for t in range(0, rows + 8, 24):
                mid, laps = lap_rows(s_ref, 7 + t, 24, tiles + 1)
                for k in range(tiles + 1):
                    kept = laps[k] * mask_ref[k // tiles, pl.ds(t, 24)]
                    q_ref[k, pl.ds(t, 24)] = a * mid[k] + b * kept
            for t in range(0, rows, 16):
                _, laps = lap_rows(q_ref, 1 + t, 16, tiles)
                for k in range(tiles):
                    spot = (n, pl.ds(t, 16), pl.ds(128 * k, 128))
                    out_ref[spot] = out_ref[spot] + w_ref[spot] + laps[k]

        return carry

    lax.fori_loop(0, beams, beam, 0)


def share_kernel(
    row_n, col_n, sums_ref, first_ref, final_ref, out_ref, halo_ref,
    held, got, left_in, right_in, corner_up, corner_down, corner_top, corner_bottom,
    send, recv, edge_send, edge_recv
):
    row, col = lax.axis_index("row"), lax.axis_index("col")
    blocks = first_ref.shape[0]

    def partner(me, hop):
        return me + hop - 2 * hop * lax.rem(lax.div(me, hop), 2)

    hops = []
    for hop in [1 << k for k in range(row_n.bit_length() - 1)]:
        hops.append((partner(row, hop), col))
    for hop in [1 << k for k in range(col_n.bit_length() - 1)]:
        hops.append((row, partner(col, hop)))
    right = (row, lax.rem(col + 1, col_n))
    left = (row, lax.rem(col + col_n - 1, col_n))
    below = (lax.rem(row + 1, row_n), col)
    above = (lax.rem(row + row_n - 1, row_n), col)

    barrier = pltpu.get_barrier_semaphore()
    others = hops + [right, left, below, above]
    for other in others:
        pl.semaphore_signal(barrier, inc=1, device_id=other, device_id_type=pl.DeviceIdType.MESH)
    pl.semaphore_wait(barrier, len(others))

    def copy(src, dst, s, r, device):
        return pltpu.make_async_remote_copy(
            src_ref=src, dst_ref=dst, send_sem=s, recv_sem=r, device_id=device,
            device_id_type=pl.DeviceIdType.MESH,
        )

    to_right = copy(final_ref, left_in, edge_send.at[0], edge_recv.at[0], right)
    to_left = copy(first_ref, right_in, edge_send.at[1], edge_recv.at[1], left)
    held[0] = sums_ref[...]
    for k, other in enumerate(hops):
        move = copy(held.at[k], got.at[k], send.at[k], recv.at[k], other)
        move.start()
        if k == 0:
            to_right.start()
            to_left.start()
        move.wait()
        held[k + 1] = held[k] + got[k]
    out_ref[...] = held[len(hops)]

    to_right.wait()
    to_left.wait()
    halo_ref[pl.ds(1, blocks), pl.ds(0, 2)] = jnp.where(col > 0, left_in[...], 0.0)
    halo_ref[pl.ds(1, blocks), pl.ds(2, 2)] = jnp.where(col < col_n - 1, right_in[...], 0.0)
    corner_up[...] = halo_ref[1]
    corner_down[...] = halo_ref[blocks]
    down = copy(corner_down, corner_top, edge_send.at[2], edge_recv.at[2], below)
    up = copy(corner_up, corner_bottom, edge_send.at[3], edge_recv.at[3], above)
    down.start()
    up.start()
    down.wait()
    up.wait()
    halo_ref[0] = jnp.where(row > 0, corner_top[...], 0.0)
    halo_ref[blocks + 1] = jnp.where(row < row_n - 1, corner_bottom[...], 0.0)


def share(sums, first, final):
    row_n, col_n = lax.axis_size("row"), lax.axis_size("col")
    blocks, _, length = first.shape
    hops = row_n.bit_length() + col_n.bit_length() - 2
    vmem = pl.BlockSpec(memory_space=pltpu.VMEM)
    return pl.pallas_call(
        functools.partial(share_kernel, row_n, col_n),
        in_specs=[vmem] * 3,
        out_specs=[vmem] * 2,
        out_shape=[jax.ShapeDtypeStruct(sums.shape, F32), jax.ShapeDtypeStruct((blocks + 2, 4, length), F32)],
        scratch_shapes=[
            pltpu.VMEM((hops + 1, *sums.shape), F32),
            pltpu.VMEM((hops, *sums.shape), F32),
            pltpu.VMEM(first.shape, F32),
            pltpu.VMEM(first.shape, F32),
            *[pltpu.VMEM((4, length), F32) for _ in range(4)],
            pltpu.SemaphoreType.DMA((hops,)),
            pltpu.SemaphoreType.DMA((hops,)),
            pltpu.SemaphoreType.DMA((4,)),
            pltpu.SemaphoreType.DMA((4,)),
        ],
        compiler_params=pltpu.CompilerParams(
            collective_id=0, has_side_effects=True, vmem_limit_bytes=LIMIT
        ),
        cost_estimate=pl.CostEstimate(flops=10**6, bytes_accessed=10**7, transcendentals=0),
        name="share",
    )(sums, first, final)


def shift_pair(first, final, axis):
    count = lax.axis_size(axis)
    up = [(i, i + 1) for i in range(count - 1)]
    down = [(i + 1, i) for i in range(count - 1)]
    return lax.ppermute(final, axis, up), lax.ppermute(first, axis, down)


def body(rows, weights, pool, desired, plan, beam_ref, step_size, smoothing, active):
    beams, height, cols = weights.shape
    count = pool.shape[0]
    blocks = height // rows
    eighths = rows // 8
    row_n, col_n = lax.axis_size("row"), lax.axis_size("col")
    row_i, col_i = lax.axis_index("row"), lax.axis_index("col")
    scale = 1.0 / math.sqrt(height * row_n * cols * col_n)
    high = lax.Precision.HIGHEST

    xt, xb = shift_pair(pool[:, :8], pool[:, -8:], "row")
    xl, xr = shift_pair(pool[:, :, 0], pool[:, :, -1], "col")
    lane = jnp.arange(128)[None, None, :]
    xe = jnp.where(lane == 0, xr[:, :, None], jnp.where(lane == 127, xl[:, :, None], 0.0))
    wt, wb = shift_pair(weights[:, :8], weights[:, -8:], "row")

    def block(n, r=rows, w=cols):
        return pl.BlockSpec((n, r, w), lambda i: (0, i, 0))

    def previous(n):
        return pl.BlockSpec((n, 8, cols), lambda i: (0, jnp.maximum(i * eighths - 1, 0), 0))

    def following(n):
        return pl.BlockSpec((n, 8, cols), lambda i: (0, jnp.minimum((i + 1) * eighths, blocks * eighths - 1), 0))

    def whole(*shape):
        return pl.BlockSpec(shape, lambda i: (0,) * len(shape))

    edges = pl.BlockSpec((1, 2, beams * rows), lambda i: (i, 0, 0))
    planes = -(-(beams + count) // 8) * 8
    sums, lx, first, final = pl.pallas_call(
        moments_kernel,
        grid=(blocks,),
        in_specs=[block(beams), block(count), previous(count), following(count), whole(count, 8, cols),
                  whole(count, 8, cols), block(count, rows, 128)],
        out_specs=[whole(planes, 128), block(count), edges, edges],
        out_shape=[
            jax.ShapeDtypeStruct((planes, 128), F32),
            jax.ShapeDtypeStruct(pool.shape, F32),
            jax.ShapeDtypeStruct((blocks, 2, beams * rows), F32),
            jax.ShapeDtypeStruct((blocks, 2, beams * rows), F32),
        ],
        scratch_shapes=[pltpu.VMEM(((beams + count) * 8, 2 * count * 8), F32)],
        compiler_params=pltpu.CompilerParams(vmem_limit_bytes=LIMIT),
        cost_estimate=pl.CostEstimate(flops=10**10, bytes_accessed=10**8, transcendentals=0),
        name="moments",
    )(weights, pool, pool, pool, xt, xb, xe)

    sums, halo = share(sums, first, final)
    gram, lapped, cross = sums[:beams, :count], sums[:beams, count : 2 * count], sums[beams : beams + count, :count]
    refs = desired.shape[1]
    pick = (beam_ref[:, None] == jnp.arange(refs, dtype=jnp.int32)[None, :]).astype(F32)
    targets = jnp.dot(pick, desired.T, precision=high)
    rate = (step_size * scale)[:, None]
    chosen = [(plan[t][None, :] == jnp.arange(count, dtype=jnp.int32)[:, None]).astype(F32) for t in range(2)]
    live = [(active > t).astype(F32)[:, None] for t in range(2)]
    s0, s1 = (live[t] * smoothing[:, None] for t in range(2))

    error0 = jnp.dot(targets - scale * gram, chosen[0], precision=high)
    c0 = live[0] * rate * jnp.dot(error0, chosen[0].T, precision=high)
    later = gram + s0 * lapped + jnp.dot(c0, cross, precision=high)
    error1 = jnp.dot(targets - scale * later, chosen[1], precision=high)
    c1 = live[1] * rate * jnp.dot(error1, chosen[1].T, precision=high)

    mix = jnp.concatenate([c0 + c1, s1 * c0], axis=1)
    flags = jnp.stack([row_i > 0, row_i < row_n - 1, col_i > 0, col_i < col_n - 1]).astype(F32)

    smem = pl.BlockSpec(memory_space=pltpu.SMEM)
    out = pl.pallas_call(
        update_kernel,
        grid=(blocks,),
        in_specs=[smem, smem, smem, block(beams), previous(beams), following(beams), whole(beams, 8, cols),
                  whole(beams, 8, cols), whole(blocks + 2, 4, beams * rows), block(count), block(count),
                  whole(beams, 2 * count)],
        out_specs=block(beams),
        out_shape=jax.ShapeDtypeStruct(weights.shape, F32),
        scratch_shapes=[
            pltpu.VMEM((3, beams, rows, 128), F32),
            pltpu.VMEM((2, rows + 8, 128), F32),
            pltpu.VMEM((beams * 8, 6 * count * 8), BF16),
            pltpu.VMEM((cols // 128 + 1, rows + 16, 128), F32),
            pltpu.VMEM((cols // 128 + 1, rows + 8, 128), F32),
        ],
        compiler_params=pltpu.CompilerParams(vmem_limit_bytes=LIMIT),
        cost_estimate=pl.CostEstimate(flops=10**10, bytes_accessed=10**8, transcendentals=0),
        name="update",
    )((s0 + s1)[:, 0], (s0 * s1)[:, 0], flags, weights, weights, weights, wt, wb, halo, pool, lx, mix)
    return out, jnp.stack([error0, error1])


def solution(mesh):
    in_specs = (P(None, "row", "col"), P(None, "row", "col"), P(), P(), P(), P(), P(), P())
    out_specs = (P(None, "row", "col"), P())
    return jax.shard_map(functools.partial(body, 64), mesh=mesh, in_specs=in_specs, out_specs=out_specs, check_vma=False)
```

```python
import functools
import math

import jax
import jax.numpy as jnp
from jax import lax
from jax.experimental import pallas as pl
from jax.experimental.pallas import tpu as pltpu
from jax.sharding import PartitionSpec as P

F32 = jnp.float32
BF16 = jnp.bfloat16
NT = (((1,), (1,)), ((), ()))
LIMIT = 56 * 1024 * 1024


def split(x):
    hi = x.astype(BF16)
    lo = (x - hi.astype(F32)).astype(BF16)
    return hi, lo


def neighbours(x, axis):
    size = x.shape[axis]
    return pltpu.roll(x, 1, axis) + pltpu.roll(x, size - 1, axis)


def one_hot(rows, cols, hit):
    r = lax.broadcasted_iota(jnp.int32, (rows, cols), 0)
    c = lax.broadcasted_iota(jnp.int32, (rows, cols), 1)
    return jnp.where(hit(r, c), 1.0, 0.0).astype(F32)


def edge(tile, lane):
    pick = one_hot(8, 128, lambda r, c: c == r + lane).astype(BF16)
    h, m = split(tile)
    l = (tile - h.astype(F32) - m.astype(F32)).astype(BF16)
    return (
        lax.dot_general(pick, h, NT, preferred_element_type=F32)
        + lax.dot_general(pick, m, NT, preferred_element_type=F32)
        + lax.dot_general(pick, l, NT, preferred_element_type=F32)
    )[:2]


def widen(raw):
    h = raw.astype(BF16).astype(F32)
    m = (raw - h).astype(BF16).astype(F32)
    l = raw - h - m
    stack = jnp.concatenate([h, m, l, jnp.zeros_like(h)], axis=0)
    r = lax.broadcasted_iota(jnp.int32, (16, 128), 0)
    c = lax.broadcasted_iota(jnp.int32, (16, 128), 1)
    k = r % 4
    spot = jnp.where(k < 2, k + 126, k - 2)
    place = jnp.where((c == spot) & (r < 12), 1.0, 0.0).astype(BF16)
    return jnp.dot(stack.T.astype(BF16), place, preferred_element_type=F32)


def remote(src, dst, s, r, device):
    return pltpu.make_async_remote_copy(
        src_ref=src, dst_ref=dst, send_sem=s, recv_sem=r, device_id=device,
        device_id_type=pl.DeviceIdType.MESH,
    )


def greet(others):
    barrier = pltpu.get_barrier_semaphore()
    for other in others:
        pl.semaphore_signal(barrier, inc=1, device_id=other, device_id_type=pl.DeviceIdType.MESH)
    pl.semaphore_wait(barrier, len(others))


def around(row, col, row_n, col_n):
    right = (row, lax.rem(col + 1, col_n))
    left = (row, lax.rem(col + col_n - 1, col_n))
    below = (lax.rem(row + 1, row_n), col)
    above = (lax.rem(row + row_n - 1, row_n), col)
    return right, left, below, above


def pool_kernel(
    row_n, col_n, x_ref, xt_ref, xb_ref, xe_ref,
    near, far, first, final, left_in, right_in, top_in, bottom_in, local, send, recv
):
    row, col = lax.axis_index("row"), lax.axis_index("col")
    pool, height, cols = x_ref.shape
    right, left, below, above = around(row, col, row_n, col_n)
    get_near = pltpu.make_async_copy(x_ref.at[:, :, pl.ds(0, 128)], near, local.at[0])
    get_far = pltpu.make_async_copy(x_ref.at[:, :, pl.ds(cols - 128, 128)], far, local.at[1])
    get_near.start()
    get_far.start()
    greet([right, left, below, above])
    down = remote(x_ref.at[:, pl.ds(height - 8, 8)], top_in, send.at[0], recv.at[0], below)
    up = remote(x_ref.at[:, pl.ds(0, 8)], bottom_in, send.at[1], recv.at[1], above)
    down.start()
    up.start()
    get_near.wait()
    first[...] = edge(near[...].reshape(pool * height, 128), 0)
    to_left = remote(first, right_in, send.at[2], recv.at[2], left)
    to_left.start()
    get_far.wait()
    final[...] = edge(far[...].reshape(pool * height, 128), 126)
    to_right = remote(final, left_in, send.at[3], recv.at[3], right)
    to_right.start()
    down.wait()
    up.wait()
    xt_ref[...] = jnp.where(row > 0, top_in[...], 0.0)
    xb_ref[...] = jnp.where(row < row_n - 1, bottom_in[...], 0.0)
    to_left.wait()
    to_right.wait()
    before = jnp.where(col > 0, left_in[...], 0.0)
    after = jnp.where(col < col_n - 1, right_in[...], 0.0)
    xe_ref[...] = widen(jnp.concatenate([before, after], axis=0)).reshape(xe_ref.shape)


def pool_halos(pool):
    row_n, col_n = lax.axis_size("row"), lax.axis_size("col")
    count, height, cols = pool.shape
    vmem = pl.BlockSpec(memory_space=pltpu.VMEM)
    strip = pltpu.VMEM((count, height, 128), F32)
    line = pltpu.VMEM((2, count * height), F32)
    slab = pltpu.VMEM((count, 8, cols), F32)
    return pl.pallas_call(
        functools.partial(pool_kernel, row_n, col_n),
        in_specs=[pl.BlockSpec(memory_space=pl.ANY)],
        out_specs=[vmem] * 3,
        out_shape=[
            jax.ShapeDtypeStruct((count, 8, cols), F32),
            jax.ShapeDtypeStruct((count, 8, cols), F32),
            jax.ShapeDtypeStruct((count, height, 128), F32),
        ],
        scratch_shapes=[
            strip, strip, line, line, line, line, slab, slab,
            pltpu.SemaphoreType.DMA((2,)), pltpu.SemaphoreType.DMA((4,)), pltpu.SemaphoreType.DMA((4,)),
        ],
        compiler_params=pltpu.CompilerParams(collective_id=1, has_side_effects=True, vmem_limit_bytes=LIMIT),
        cost_estimate=pl.CostEstimate(flops=10**6, bytes_accessed=10**7, transcendentals=0),
        name="pool_halos",
    )(pool)


def moments_kernel(w_ref, x_ref, xp_ref, xn_ref, xt_ref, xb_ref, xe_ref, out_ref, lx_ref, el_ref, er_ref, acc_ref):
    i, last = pl.program_id(0), pl.num_programs(0) - 1
    beams, rows, cols = w_ref.shape
    pool = x_ref.shape[0]

    @pl.when(i == 0)
    def _():
        acc_ref[...] = jnp.zeros_like(acc_ref)

    for p in range(pool):
        above = jnp.where(i == 0, xt_ref[p], xp_ref[p])
        below = jnp.where(i == last, xb_ref[p], xn_ref[p])
        cur = x_ref[p]
        tall = jnp.concatenate([above, cur, below], axis=0)
        wide = jnp.concatenate([cur, xe_ref[p]], axis=1)
        lx_ref[p] = neighbours(tall, 0)[8 : rows + 8] + neighbours(wide, 1)[:, :cols] - 4.0 * cur

    for g in range(rows // 8):
        part = pl.ds(8 * g, 8)
        wg = w_ref[:, part, :].reshape(beams * 8, cols)
        xg = x_ref[:, part, :].reshape(pool * 8, cols)
        lg = lx_ref[:, part, :].reshape(pool * 8, cols)
        lh, ll = split(jnp.concatenate([wg, xg], axis=0))
        rh, rl = split(jnp.concatenate([xg, lg], axis=0))
        left = jnp.concatenate([lh, ll, lh], axis=1)
        right = jnp.concatenate([rh, rh, rl], axis=1)
        acc_ref[...] += lax.dot_general(left, right, NT, preferred_element_type=F32)

    el_ref[0] = edge(w_ref[:, :, :128].reshape(beams * rows, 128), 0)
    er_ref[0] = edge(w_ref[:, :, cols - 128 :].reshape(beams * rows, 128), 126)

    @pl.when(i == last)
    def _():
        n, m = acc_ref.shape
        kept = acc_ref[...] * one_hot(n, m, lambda r, c: r % 8 == c % 8)
        fold = one_hot(m, 128, lambda r, c: r // 8 == c)
        gather = one_hot(out_ref.shape[0], n, lambda r, c: c // 8 == r)
        half = jnp.dot(kept, fold, precision=lax.Precision.HIGHEST, preferred_element_type=F32)
        out_ref[...] = jnp.dot(gather, half, precision=lax.Precision.HIGHEST, preferred_element_type=F32)


def update_kernel(
    a_ref, b_ref, flag_ref, w_ref, wp_ref, wn_ref, wt_ref, wb_ref, halo_ref, x_ref, lx_ref, coef_ref,
    out_ref, tile_ref, mask_ref, mix_ref, s_ref, q_ref
):
    i, last = pl.program_id(0), pl.num_programs(0) - 1
    beams, rows, cols = w_ref.shape
    pool = x_ref.shape[0]
    tiles = cols // 128

    def make_tile(j):
        tile = widen(halo_ref[j])
        tile_ref[j % 3] = tile.reshape(beams, rows, 128)

    @pl.when(i == 0)
    def _():
        make_tile(0)
        make_tile(1)
        n, m = beams * 8, 2 * pool * 8
        down = one_hot(n, beams, lambda r, c: r // 8 == c)
        along = one_hot(2 * pool, m, lambda r, c: r == c // 8)
        full = jnp.dot(down, coef_ref[...], precision=lax.Precision.HIGHEST, preferred_element_type=F32)
        full = jnp.dot(full, along, precision=lax.Precision.HIGHEST, preferred_element_type=F32)
        high, low = split(full * one_hot(n, m, lambda r, c: r % 8 == c % 8))
        mix_ref[...] = jnp.concatenate([high, high, low], axis=1)

    make_tile(i + 2)

    r = lax.broadcasted_iota(jnp.int32, (rows + 8, 128), 0)
    c = lax.broadcasted_iota(jnp.int32, (rows + 8, 128), 1)
    mask = jnp.where((r == 0) & (i == 0), flag_ref[0], 1.0)
    mask = jnp.where((r == rows + 1) & (i == last), flag_ref[1], mask)
    mask_ref[0] = mask
    mask_ref[1] = mask * jnp.where(c >= 64, flag_ref[2], flag_ref[3])

    for g in range(rows // 8):
        part = pl.ds(8 * g, 8)
        xg = x_ref[:, part, :].reshape(pool * 8, cols)
        lg = lx_ref[:, part, :].reshape(pool * 8, cols)
        rh, rl = split(jnp.concatenate([xg, lg], axis=0))
        full = jnp.concatenate([rh, rl, rh], axis=0)
        mixed = jnp.dot(mix_ref[...], full, preferred_element_type=F32)
        out_ref[:, part, :] = mixed.reshape(beams, 8, cols)

    before, here, after = lax.rem(i, 3), lax.rem(i + 1, 3), lax.rem(i + 2, 3)

    def across(parts, count):
        lane = lax.broadcasted_iota(jnp.int32, parts[0].shape, 1)
        one = [pltpu.roll(v, 1, 1) for v in parts]
        two = [pltpu.roll(v, 127, 1) for v in parts]
        n = len(parts)
        return [
            jnp.where(lane == 0, one[k - 1], one[k]) + jnp.where(lane == 127, two[(k + 1) % n], two[k])
            for k in range(count)
        ]

    def lap_rows(ref, start, size, count):
        mid = [ref[k, pl.ds(start, size)] for k in range(tiles + 1)]
        side = across(mid, count)
        laps = [
            ref[k, pl.ds(start - 1, size)] + ref[k, pl.ds(start + 1, size)] + side[k] - 4.0 * mid[k]
            for k in range(count)
        ]
        return mid, laps

    def beam(n, carry):
        a, b = a_ref[n], b_ref[n]
        for k in range(tiles):
            lanes = pl.ds(128 * k, 128)
            s_ref[k, pl.ds(0, 8)] = jnp.where(i == 0, wt_ref[n, :, lanes] * flag_ref[0], wp_ref[n, :, lanes])
            s_ref[k, pl.ds(8, rows)] = w_ref[n, :, lanes]
            s_ref[k, pl.ds(rows + 8, 8)] = jnp.where(i == last, wb_ref[n, :, lanes] * flag_ref[1], wn_ref[n, :, lanes])
        s_ref[tiles, pl.ds(0, 8)] = tile_ref[before, n, pl.ds(rows - 8, 8)]
        s_ref[tiles, pl.ds(8, rows)] = tile_ref[here, n]
        s_ref[tiles, pl.ds(rows + 8, 8)] = tile_ref[after, n, pl.ds(0, 8)]

        @pl.when(b == 0.0)
        def _():
            for t in range(0, rows, 16):
                mid, laps = lap_rows(s_ref, 8 + t, 16, tiles)
                for k in range(tiles):
                    spot = (n, pl.ds(t, 16), pl.ds(128 * k, 128))
                    out_ref[spot] = out_ref[spot] + mid[k] + a * laps[k]

        @pl.when(b != 0.0)
        def _():
            for t in range(0, rows + 8, 24):
                mid, laps = lap_rows(s_ref, 7 + t, 24, tiles + 1)
                for k in range(tiles + 1):
                    kept = laps[k] * mask_ref[k // tiles, pl.ds(t, 24)]
                    q_ref[k, pl.ds(t, 24)] = a * mid[k] + b * kept
            for t in range(0, rows, 16):
                _, laps = lap_rows(q_ref, 1 + t, 16, tiles)
                for k in range(tiles):
                    spot = (n, pl.ds(t, 16), pl.ds(128 * k, 128))
                    out_ref[spot] = out_ref[spot] + w_ref[spot] + laps[k]

        return carry

    lax.fori_loop(0, beams, beam, 0)


def share_kernel(
    row_n, col_n, w_ref, sums_ref, first_ref, final_ref, wt_ref, wb_ref, out_ref, halo_ref,
    row_got, col_got, part, left_in, right_in, corner_up, corner_down, corner_top, corner_bottom,
    send, recv, edge_send, edge_recv
):
    row, col = lax.axis_index("row"), lax.axis_index("col")
    blocks = first_ref.shape[0]
    height = w_ref.shape[1]
    right, left, below, above = around(row, col, row_n, col_n)
    row_peers = [(lax.rem(row + d, row_n), col) for d in range(1, row_n)]
    col_peers = [(row, lax.rem(col + d, col_n)) for d in range(1, col_n)]
    greet(row_peers + col_peers)

    gather = [
        remote(sums_ref, row_got.at[row], send.at[k], recv.at[k], peer) for k, peer in enumerate(row_peers)
    ]
    to_right = remote(final_ref, left_in, edge_send.at[0], edge_recv.at[0], right)
    to_left = remote(first_ref, right_in, edge_send.at[1], edge_recv.at[1], left)
    w_down = remote(w_ref.at[:, pl.ds(height - 8, 8)], wt_ref, edge_send.at[4], edge_recv.at[4], below)
    w_up = remote(w_ref.at[:, pl.ds(0, 8)], wb_ref, edge_send.at[5], edge_recv.at[5], above)
    for move in gather + [to_right, to_left, w_down, w_up]:
        move.start()
    row_got[row] = sums_ref[...]
    for move in gather:
        move.wait()
    value = row_got[0]
    for k in range(1, row_n):
        value = value + row_got[k]
    part[...] = value
    base = row_n - 1
    spread = [
        remote(part, col_got.at[col], send.at[base + k], recv.at[base + k], peer)
        for k, peer in enumerate(col_peers)
    ]
    for move in spread:
        move.start()
    col_got[col] = value

    to_right.wait()
    to_left.wait()
    halo_ref[pl.ds(1, blocks), pl.ds(0, 2)] = jnp.where(col > 0, left_in[...], 0.0)
    halo_ref[pl.ds(1, blocks), pl.ds(2, 2)] = jnp.where(col < col_n - 1, right_in[...], 0.0)
    corner_up[...] = halo_ref[1]
    corner_down[...] = halo_ref[blocks]
    down = remote(corner_down, corner_top, edge_send.at[2], edge_recv.at[2], below)
    up = remote(corner_up, corner_bottom, edge_send.at[3], edge_recv.at[3], above)
    down.start()
    up.start()

    for move in spread:
        move.wait()
    value = col_got[0]
    for k in range(1, col_n):
        value = value + col_got[k]
    out_ref[...] = value
    down.wait()
    up.wait()
    halo_ref[0] = jnp.where(row > 0, corner_top[...], 0.0)
    halo_ref[blocks + 1] = jnp.where(row < row_n - 1, corner_bottom[...], 0.0)
    w_down.wait()
    w_up.wait()


def share(weights, sums, first, final):
    row_n, col_n = lax.axis_size("row"), lax.axis_size("col")
    beams, _, cols = weights.shape
    blocks, _, length = first.shape
    moves = row_n + col_n - 2
    vmem = pl.BlockSpec(memory_space=pltpu.VMEM)
    hbm = pl.BlockSpec(memory_space=pl.ANY)
    slab = jax.ShapeDtypeStruct((beams, 8, cols), F32)
    return pl.pallas_call(
        functools.partial(share_kernel, row_n, col_n),
        in_specs=[hbm] + [vmem] * 3,
        out_specs=[hbm, hbm, vmem, vmem],
        out_shape=[
            slab, slab,
            jax.ShapeDtypeStruct(sums.shape, F32),
            jax.ShapeDtypeStruct((blocks + 2, 4, length), F32),
        ],
        scratch_shapes=[
            pltpu.VMEM((row_n, *sums.shape), F32),
            pltpu.VMEM((col_n, *sums.shape), F32),
            pltpu.VMEM(sums.shape, F32),
            pltpu.VMEM(first.shape, F32),
            pltpu.VMEM(first.shape, F32),
            *[pltpu.VMEM((4, length), F32) for _ in range(4)],
            pltpu.SemaphoreType.DMA((moves,)),
            pltpu.SemaphoreType.DMA((moves,)),
            pltpu.SemaphoreType.DMA((6,)),
            pltpu.SemaphoreType.DMA((6,)),
        ],
        compiler_params=pltpu.CompilerParams(
            collective_id=0, has_side_effects=True, vmem_limit_bytes=LIMIT
        ),
        cost_estimate=pl.CostEstimate(flops=10**6, bytes_accessed=10**7, transcendentals=0),
        name="share",
    )(weights, sums, first, final)


def body(rows, weights, pool, desired, plan, beam_ref, step_size, smoothing, active):
    beams, height, cols = weights.shape
    count = pool.shape[0]
    blocks = height // rows
    eighths = rows // 8
    row_n, col_n = lax.axis_size("row"), lax.axis_size("col")
    row_i, col_i = lax.axis_index("row"), lax.axis_index("col")
    scale = 1.0 / math.sqrt(height * row_n * cols * col_n)
    high = lax.Precision.HIGHEST

    xt, xb, xe = pool_halos(pool)

    def block(n, r=rows, w=cols):
        return pl.BlockSpec((n, r, w), lambda i: (0, i, 0))

    def previous(n):
        return pl.BlockSpec((n, 8, cols), lambda i: (0, jnp.maximum(i * eighths - 1, 0), 0))

    def following(n):
        return pl.BlockSpec((n, 8, cols), lambda i: (0, jnp.minimum((i + 1) * eighths, blocks * eighths - 1), 0))

    def whole(*shape):
        return pl.BlockSpec(shape, lambda i: (0,) * len(shape))

    edges = pl.BlockSpec((1, 2, beams * rows), lambda i: (i, 0, 0))
    planes = -(-(beams + count) // 8) * 8
    sums, lx, first, final = pl.pallas_call(
        moments_kernel,
        grid=(blocks,),
        in_specs=[block(beams), block(count), previous(count), following(count), whole(count, 8, cols),
                  whole(count, 8, cols), block(count, rows, 128)],
        out_specs=[whole(planes, 128), block(count), edges, edges],
        out_shape=[
            jax.ShapeDtypeStruct((planes, 128), F32),
            jax.ShapeDtypeStruct(pool.shape, F32),
            jax.ShapeDtypeStruct((blocks, 2, beams * rows), F32),
            jax.ShapeDtypeStruct((blocks, 2, beams * rows), F32),
        ],
        scratch_shapes=[pltpu.VMEM(((beams + count) * 8, 2 * count * 8), F32)],
        compiler_params=pltpu.CompilerParams(vmem_limit_bytes=LIMIT),
        cost_estimate=pl.CostEstimate(flops=10**10, bytes_accessed=10**8, transcendentals=0),
        name="moments",
    )(weights, pool, pool, pool, xt, xb, xe)

    wt, wb, sums, halo = share(weights, sums, first, final)
    gram, lapped, cross = sums[:beams, :count], sums[:beams, count : 2 * count], sums[beams : beams + count, :count]
    refs = desired.shape[1]
    pick = (beam_ref[:, None] == jnp.arange(refs, dtype=jnp.int32)[None, :]).astype(F32)
    targets = jnp.dot(pick, desired.T, precision=high)
    rate = (step_size * scale)[:, None]
    chosen = [(plan[t][None, :] == jnp.arange(count, dtype=jnp.int32)[:, None]).astype(F32) for t in range(2)]
    live = [(active > t).astype(F32)[:, None] for t in range(2)]
    s0, s1 = (live[t] * smoothing[:, None] for t in range(2))

    error0 = jnp.dot(targets - scale * gram, chosen[0], precision=high)
    c0 = live[0] * rate * jnp.dot(error0, chosen[0].T, precision=high)
    later = gram + s0 * lapped + jnp.dot(c0, cross, precision=high)
    error1 = jnp.dot(targets - scale * later, chosen[1], precision=high)
    c1 = live[1] * rate * jnp.dot(error1, chosen[1].T, precision=high)

    mix = jnp.concatenate([c0 + c1, s1 * c0], axis=1)
    flags = jnp.stack([row_i > 0, row_i < row_n - 1, col_i > 0, col_i < col_n - 1]).astype(F32)

    smem = pl.BlockSpec(memory_space=pltpu.SMEM)
    out = pl.pallas_call(
        update_kernel,
        grid=(blocks,),
        in_specs=[smem, smem, smem, block(beams), previous(beams), following(beams), whole(beams, 8, cols),
                  whole(beams, 8, cols), whole(blocks + 2, 4, beams * rows), block(count), block(count),
                  whole(beams, 2 * count)],
        out_specs=block(beams),
        out_shape=jax.ShapeDtypeStruct(weights.shape, F32),
        scratch_shapes=[
            pltpu.VMEM((3, beams, rows, 128), F32),
            pltpu.VMEM((2, rows + 8, 128), F32),
            pltpu.VMEM((beams * 8, 6 * count * 8), BF16),
            pltpu.VMEM((cols // 128 + 1, rows + 16, 128), F32),
            pltpu.VMEM((cols // 128 + 1, rows + 8, 128), F32),
        ],
        compiler_params=pltpu.CompilerParams(vmem_limit_bytes=LIMIT),
        cost_estimate=pl.CostEstimate(flops=10**10, bytes_accessed=10**8, transcendentals=0),
        name="update",
    )((s0 + s1)[:, 0], (s0 * s1)[:, 0], flags, weights, weights, weights, wt, wb, halo, pool, lx, mix)
    return out, jnp.stack([error0, error1])


def solution(mesh):
    in_specs = (P(None, "row", "col"), P(None, "row", "col"), P(), P(), P(), P(), P(), P())
    out_specs = (P(None, "row", "col"), P())
    return jax.shard_map(functools.partial(body, 64), mesh=mesh, in_specs=in_specs, out_specs=out_specs, check_vma=False)
```
